32 devices in a mesh: fsdp: 16 (over z, y, core), tp: 2 (over x).
Axes of the slice: x: 2, y: 2, z: 4, core: 2. Of those that a mesh axis runs over, the one named last changes fastest.
Arguments:
- tokens: bfloat16 [16384, 1024], P(('fsdp', 'tp')), may hold values from -6 to 6
- cotangent: bfloat16 [16384, 1024], P(('fsdp', 'tp')), may hold values from -6 to 6
- qkv_weight: bfloat16 [1024, 3, 1024], P('fsdp', None, 'tp'), may hold values from -0.1875 to 0.1875
- qkv_bias: float32 [3, 1024], P(None, 'tp'), may hold values from -0.3 to 0.3
- out_weight: bfloat16 [1024, 1024], P('fsdp', 'tp'), may hold values from -1.5 to 1.5
- out_bias: float32 [1024], replicated, may hold values from -1.8 to 1.8
- up_weight: bfloat16 [1024, 4096], P('fsdp', 'tp'), may hold values from -0.1875 to 0.1875
- up_bias: float32 [4096], P('tp'), may hold values from -1.8 to 1.8
- down_weight: bfloat16 [1024, 4096], P('fsdp', 'tp'), may hold values from -0.09375 to 0.09375
- down_bias: float32 [1024], replicated, may hold values from -1.8 to 1.8
- attn_gain: float32 [1024], replicated, may hold values from 0.25 to 1.75
- attn_shift: float32 [1024], replicated, may hold values from -1.8 to 1.8
- mlp_gain: float32 [1024], replicated, may hold values from 0.25 to 1.75
- mlp_shift: float32 [1024], replicated, may hold values from -1.8 to 1.8
Outputs:
- mixed: bfloat16 [16384, 1024], P(('fsdp', 'tp'))
- tokens_grad: bfloat16 [16384, 1024], P(('fsdp', 'tp'))
- qkv_weight_grad: float32 [1024, 3, 1024], P('fsdp', None, 'tp')
- qkv_bias_grad: float32 [3, 1024], P(None, 'tp')
- out_weight_grad: float32 [1024, 1024], P('fsdp', 'tp')
- out_bias_grad: float32 [1024], replicated
- up_weight_grad: float32 [1024, 4096], P('fsdp', 'tp')
- up_bias_grad: float32 [4096], P('tp')
- down_weight_grad: float32 [1024, 4096], P('fsdp', 'tp')
- down_bias_grad: float32 [1024], replicated
- attn_gain_grad: float32 [1024], replicated
- attn_shift_grad: float32 [1024], replicated
- mlp_gain_grad: float32 [1024], replicated
- mlp_shift_grad: float32 [1024], replicated
The draws below stay inside these ranges and needn't reach their ends.
All inputs are finite; a program needn't handle non-finite values.
Results may differ from the reference program's by a relative error of at most 0.014.
Values may be sent and summed in bfloat16 or wider, within the bound.
A program may use at most 192 MiB of HBM per device.

```python
import math
import jax
import jax.numpy as jnp
from jax import lax

D = 1024
HEADS = 16
HD = 64
ROT = 16
FF = 4096
SEQ = 1024
TOKENS = 16384


def raised(values, stream_key, source, target, blocks, factor):
    def block_of(dim):
        return (jnp.arange(values.shape[dim]) // (values.shape[dim] // blocks)).reshape((-1,) + (1,) * (values.ndim - 1 - dim))

    near = jax.random.permutation(stream_key, blocks)[block_of(target)]
    second = (block_of(target) + blocks // 2) % blocks
    return jnp.where((block_of(source) == near) | (block_of(source) == second), factor * values, values)


def steps_of(stream_key, shape, cuts, low, largest):
    factor_of = 1.0
    for axis_at, parts in cuts:
        steps = jax.random.uniform(jax.random.fold_in(jax.random.fold_in(stream_key, 6), axis_at), (parts,), jnp.float32, low / len(cuts), largest / len(cuts))
        factor_of = factor_of * jnp.repeat(jnp.exp(steps), shape[axis_at] // parts).reshape((-1,) + (1,) * (len(shape) - 1 - axis_at))
    return factor_of


def normal_values(stream_key, dims, scale, limit, split=(), kind=jnp.bfloat16):
    drawn = scale * jax.random.normal(stream_key, dims, jnp.float32)
    if split:
        drawn = drawn * steps_of(stream_key, dims, split, -0.22, 0.18)
    return jnp.clip(drawn, -limit, limit).astype(kind)


def bell_draw_with(own_key, shape, scale, reach, shards, heavy, kind=jnp.bfloat16):
    values = scale * jax.random.normal(own_key, shape, jnp.float32)
    if shards:
        values = values * steps_of(own_key, shape, shards, -0.22, 0.18)
    return jnp.clip(raised(values, jax.random.fold_in(own_key, 3), *heavy), -reach, reach).astype(kind)


def setup_inputs(seed: int = 0) -> dict:
    arg_keys = jax.random.split(jax.random.key(seed), 15)
    return {
        "tokens": normal_values(arg_keys[0], (TOKENS, D), 1.0, 6.0, ((0, 32),)),
        "cotangent": bell_draw_with(arg_keys[1], (TOKENS, D), 1.0, 6.0, ((0, 32),), (0, 1, 32, 2.75)),
        "qkv_weight": normal_values(arg_keys[2], (D, 3, D), D ** -0.5, 0.1875, ((0, 16), (2, 2))),
        "qkv_bias": normal_values(arg_keys[3], (3, D), 0.05, 0.3, ((1, 2),), jnp.float32),
        "out_weight": normal_values(arg_keys[4], (D, D), (D // 64) ** -0.5, 1.5, ((0, 16), (1, 2))),
        "out_bias": normal_values(arg_keys[5], (D,), 0.3, 1.8, (), jnp.float32),
        "up_weight": normal_values(arg_keys[6], (D, FF), D ** -0.5, 0.1875, ((0, 16), (1, 2))),
        "up_bias": normal_values(arg_keys[7], (FF,), 0.3, 1.8, ((0, 2),), jnp.float32),
        "down_weight": normal_values(arg_keys[8], (D, FF), FF ** -0.5, 0.09375, ((0, 16), (1, 2))),
        "down_bias": normal_values(arg_keys[9], (D,), 0.3, 1.8, (), jnp.float32),
        "attn_gain": jnp.clip(1.0 + 0.15 * jax.random.normal(arg_keys[10], (D,), jnp.float32), 0.25, 1.75),
        "attn_shift": normal_values(arg_keys[11], (D,), 0.3, 1.8, (), jnp.float32),
        "mlp_gain": jnp.clip(1.0 + 0.15 * jax.random.normal(arg_keys[12], (D,), jnp.float32), 0.25, 1.75),
        "mlp_shift": normal_values(arg_keys[13], (D,), 0.3, 1.8, (), jnp.float32),
    }


EPS = 1e-05
MASKED = -1e+30
BASE = 10000.0
HIGH = lax.Precision.HIGHEST

@jax.custom_vjp
def low(v):
    return lax.optimization_barrier(v.astype(jnp.bfloat16)).astype(jnp.float32)

@jax.custom_vjp
def low_back(v):
    return v

def low_keep(v):
    return (low(v), None)

def low_pass(kept, grad):
    return (grad,)

def back_keep(v):
    return (v, None)

def back_low(kept, grad):
    return (low(grad),)
low.defvjp(low_keep, low_pass)
low_back.defvjp(back_keep, back_low)

def norm_rows(values):
    center = values - lax.optimization_barrier(jnp.mean(values, axis=-1, keepdims=True))
    spread = lax.optimization_barrier(jnp.mean(center * center, axis=-1, keepdims=True))
    return center * lax.rsqrt(spread + EPS)

def rotary_tables(count):
    half = ROT // 2
    places = (jnp.arange(count, dtype=jnp.int32) % SEQ).astype(jnp.float32)
    rates = BASE ** (-2.0 * jnp.arange(half, dtype=jnp.float32) / ROT)
    angles = places[:, None] * rates[None, :]
    return (jnp.cos(angles)[:, None, :], jnp.sin(angles)[:, None, :])

def rotate(values, cosine, sine):
    half = ROT // 2
    first = values[..., :half]
    second = values[..., half:ROT]
    return jnp.concatenate([first * cosine - second * sine, second * cosine + first * sine, values[..., ROT:]], axis=-1)

def attention(queries, keys, values):
    count = queries.shape[0]
    block = min(512, SEQ)
    per_seq = SEQ // block
    scale = HD ** (-0.5)

    def one_block(index):
        seq_start = index // per_seq * SEQ
        offset = index % per_seq * block
        rows = lax.dynamic_slice_in_dim(queries, seq_start + offset, block, 0)
        key_seq = lax.dynamic_slice_in_dim(keys, seq_start, SEQ, 0)
        value_seq = lax.dynamic_slice_in_dim(values, seq_start, SEQ, 0)
        scores = low_back(jnp.einsum('qhd,khd->hqk', rows, key_seq, precision=HIGH) * scale)
        places = offset + jnp.arange(block, dtype=jnp.int32)
        allowed = jnp.arange(SEQ, dtype=jnp.int32)[None, :] <= places[:, None]
        scores = jnp.where(allowed[None], scores, MASKED)
        top = lax.optimization_barrier(jnp.max(scores, axis=-1, keepdims=True))
        expo = jnp.exp(scores - top)
        probs = low(expo / lax.optimization_barrier(jnp.sum(expo, axis=-1, keepdims=True)))
        return jnp.einsum('hqk,khd->qhd', probs, value_seq, precision=HIGH)
    blocks = lax.map(jax.checkpoint(one_block), jnp.arange(count // block, dtype=jnp.int32))
    return blocks.reshape(count, HEADS * HD)

def layer(inputs, qkv_weight, qkv_bias, out_weight, out_bias, up_weight, up_bias, down_weight, down_bias, attn_gain, attn_shift, mlp_gain, mlp_shift):
    count = inputs.shape[0]
    normal = norm_rows(inputs)
    first = low(normal * attn_gain + attn_shift)
    second = low(normal * mlp_gain + mlp_shift)
    joined = low_back(jnp.dot(first, qkv_weight.reshape(D, 3 * D), precision=HIGH, preferred_element_type=jnp.float32) + qkv_bias.reshape(3 * D))
    cosine, sine = rotary_tables(count)
    queries = low(rotate(joined[:, :D].reshape(count, HEADS, HD), cosine, sine))
    keys = low(rotate(joined[:, D:2 * D].reshape(count, HEADS, HD), cosine, sine))
    values = low(joined[:, 2 * D:].reshape(count, HEADS, HD))
    attended = low(low_back(attention(queries, keys, values)))
    pre = low_back(jnp.dot(second, up_weight, precision=HIGH, preferred_element_type=jnp.float32) + up_bias)
    activated = low(jax.nn.gelu(pre, approximate=False))
    attn_branch = jnp.dot(attended, out_weight.T, precision=HIGH, preferred_element_type=jnp.float32) + out_bias
    mlp_branch = jnp.dot(activated, down_weight.T, precision=HIGH, preferred_element_type=jnp.float32) + down_bias
    return inputs + attn_branch + mlp_branch

def reference(tokens, cotangent, qkv_weight, qkv_bias, out_weight, out_bias, up_weight, up_bias, down_weight, down_bias, attn_gain, attn_shift, mlp_gain, mlp_shift):
    params = tuple((array.astype(jnp.float32) for array in (qkv_weight, qkv_bias, out_weight, out_bias, up_weight, up_bias, down_weight, down_bias, attn_gain, attn_shift, mlp_gain, mlp_shift)))
    total = tokens.shape[0]
    group = math.gcd(total // SEQ, max(1, 4096 // SEQ)) * SEQ
    groups = total // group
    inputs = tokens.astype(jnp.float32).reshape(groups, group, D)
    grads_in = cotangent.astype(jnp.float32).reshape(groups, group, D)

    def one_group(acc, pair):
        rows, row_grads = pair
        output, pull = jax.vjp(layer, rows, *params)
        grads = pull(row_grads)
        acc = tuple((left + right for left, right in zip(acc, grads[1:])))
        return (acc, (output.astype(jnp.bfloat16), grads[0].astype(jnp.bfloat16)))
    init = tuple((jnp.zeros_like(array) for array in params))
    sums, (outputs, backs) = lax.scan(one_group, init, (inputs, grads_in))
    return (outputs.reshape(total, D), backs.reshape(total, D), sums[0], sums[1], sums[2], sums[3], sums[4], sums[5], sums[6], sums[7], sums[8], sums[9], sums[10], sums[11])
```

```python
import functools

import jax
import jax.numpy as jnp
import numpy as np
from jax import lax
from jax.experimental import pallas as pl
from jax.experimental.pallas import tpu as pltpu
from jax.sharding import PartitionSpec as P

HD = 64
ROT = 16
SEQ = 1024
QBLOCK = 256


EPS = 1e-05
MASKED = -1e30
BASE = 10000.0
LAST = (((1,), (1,)), ((), ()))
FIRST = (((0,), (0,)), ((), ()))


def norm_rows(values):
    center = values - jnp.mean(values, axis=-1, keepdims=True)
    spread = jnp.mean(center * center, axis=-1, keepdims=True)
    factor = lax.rsqrt(spread + EPS)
    return (center * factor, factor)


def rotary_tables():
    half = ROT // 2
    rates = BASE ** (-2.0 * np.arange(half) / ROT)
    angles = np.arange(SEQ)[:, None] * rates[None, :]
    cosine = np.ones((SEQ, HD), np.float32)
    right = np.zeros((SEQ, HD), np.float32)
    left = np.zeros((SEQ, HD), np.float32)
    cosine[:, :half] = cosine[:, half:ROT] = np.cos(angles)
    right[:, :half] = -np.sin(angles)
    left[:, half:ROT] = np.sin(angles)
    return tuple(np.concatenate([one, one], axis=1) for one in (cosine, right, left))


def attend_kernel(scale, q_ref, k_ref, v_ref, qb_ref, kb_ref, vb_ref, ag_ref, cos_ref, sa_ref, sb_ref,
                  att_ref, jg_ref, bias_ref, q_s, k_s, v_s, dk_s, dv_s, dq_s):
    pair = pl.program_id(0)
    cols = jg_ref.shape[1] // 3
    half = ROT // 2
    lanes = 2 * HD
    block = QBLOCK
    low = lax.broadcasted_iota(jnp.int32, (SEQ, lanes), 1) < HD

    def rotary(x, sign):
        return (
            x * cos_ref[...]
            + sign * (pltpu.roll(x, lanes - half, 1) * sa_ref[...] + pltpu.roll(x, half, 1) * sb_ref[...])
        )

    q = (rotary(q_ref[...] + qb_ref[...], 1.0).astype(jnp.bfloat16) * scale).astype(jnp.bfloat16)
    k = rotary(k_ref[...] + kb_ref[...], 1.0).astype(jnp.bfloat16)
    v = (v_ref[...] + vb_ref[...]).astype(jnp.bfloat16)
    zero = jnp.zeros((SEQ, lanes), jnp.bfloat16)
    q_s[0] = jnp.where(low, q, zero)
    q_s[1] = jnp.where(low, zero, q)
    k_s[0] = jnp.where(low, k, zero)
    k_s[1] = jnp.where(low, zero, k)
    v_s[0] = jnp.where(low, v, zero)
    v_s[1] = jnp.where(low, zero, v)
    ag = ag_ref[...]
    nt = (((1,), (1,)), ((), ()))
    tn = (((0,), (0,)), ((), ()))
    keep = lax.broadcasted_iota(jnp.int32, (block, block), 0) <= lax.broadcasted_iota(
        jnp.int32, (block, block), 1
    )
    low_block = low[:block]
    for part in range(SEQ // block):
        begin, end = part * block, (part + 1) * block
        ag_rows = ag_ref[begin:end, :]
        att = jnp.zeros((block, lanes), jnp.float32)
        dq = jnp.zeros((block, lanes), jnp.float32)
        for head in range(2):
            q_rows = q_s[head, begin:end, :]
            ag_head = jnp.where(low_block if head == 0 else ~low_block, ag_rows, jnp.zeros_like(ag_rows))
            scores = lax.dot_general(k_s[head, :end, :], q_rows, nt, preferred_element_type=jnp.float32)
            diag = jnp.where(keep, scores[begin:end], MASKED)
            scores = diag if part == 0 else jnp.concatenate([scores[:begin], diag], axis=0)
            top = jnp.max(scores, axis=0, keepdims=True)
            expo = jnp.exp(scores - top)
            inverse = 1.0 / jnp.sum(expo, axis=0, keepdims=True)
            probs = expo * inverse
            probs16 = probs.astype(jnp.bfloat16)
            att += lax.dot_general(probs16, v_s[head, :end, :], tn, preferred_element_type=jnp.float32)
            dp = lax.dot_general(v_s[head, :end, :], ag_rows, nt, preferred_element_type=jnp.float32)
            delta = jnp.sum(probs * dp, axis=0, keepdims=True)
            ds = (probs * (dp - delta)).astype(jnp.bfloat16)
            dq += lax.dot_general(ds, k_s[head, :end, :], tn, preferred_element_type=jnp.float32)
            dk = lax.dot_general(ds, q_rows, (((1,), (0,)), ((), ())), preferred_element_type=jnp.float32)
            dv = lax.dot_general(probs16, ag_head, (((1,), (0,)), ((), ())), preferred_element_type=jnp.float32)
            first = head == 0
            if first:
                if begin:
                    dk_s[:begin, :] += dk[:begin]
                    dv_s[:begin, :] += dv[:begin]
                dk_s[begin:end, :] = dk[begin:]
                dv_s[begin:end, :] = dv[begin:]
            else:
                dk_s[:end, :] += dk
                dv_s[:end, :] += dv
        att_ref[begin:end, :] = att.astype(jnp.bfloat16)
        dq_s[begin:end, :] = dq * scale
    grads = (rotary(dq_s[...], -1.0), rotary(dk_s[...], -1.0), dv_s[...])
    for which in range(3):
        value = grads[which].astype(jnp.bfloat16)
        at = pl.ds(pl.multiple_of(which * cols + pair * lanes, lanes), lanes)
        jg_ref[:, at] = value
        bias_ref[which] = jnp.sum(value.astype(jnp.float32), axis=0, keepdims=True)


def attention(joined, bias, att_grad, scale):
    rows, cols = att_grad.shape
    lanes = 2 * HD
    pairs = cols // lanes
    seqs = rows // SEQ
    tables = rotary_tables()

    def part(which):
        return pl.BlockSpec((SEQ, lanes), lambda p: (0, which * pairs + p))

    def bias_part(which):
        return pl.BlockSpec((1, lanes), lambda p: (0, which * pairs + p))

    table = pl.BlockSpec((SEQ, lanes), lambda p: (0, 0))
    big = pltpu.VMEM((2, SEQ, lanes), jnp.bfloat16)
    run = pl.pallas_call(
        functools.partial(attend_kernel, scale),
        grid=(pairs,),
        in_specs=[part(0), part(1), part(2), bias_part(0), bias_part(1), bias_part(2), part(0), table, table, table],
        out_specs=[
            part(0),
            pl.BlockSpec((SEQ, 3 * cols), lambda p: (0, 0)),
            pl.BlockSpec((3, 1, lanes), lambda p: (0, 0, p)),
        ],
        out_shape=[
            jax.ShapeDtypeStruct((SEQ, cols), jnp.bfloat16),
            jax.ShapeDtypeStruct((SEQ, 3 * cols), jnp.bfloat16),
            jax.ShapeDtypeStruct((3, 1, cols), jnp.float32),
        ],
        scratch_shapes=[big, big, big] + [pltpu.VMEM((SEQ, lanes), jnp.float32)] * 3,
        compiler_params=pltpu.CompilerParams(vmem_limit_bytes=40 * 2**20),
        cost_estimate=pl.CostEstimate(
            flops=40 * SEQ * SEQ * cols, bytes_accessed=14 * SEQ * cols, transcendentals=SEQ * SEQ * cols // HD
        ),
        name="attention",
    )
    outs = []
    for s in range(seqs):
        at = slice(s * SEQ, (s + 1) * SEQ)
        j = joined[at]
        outs.append(run(j, j, j, bias, bias, bias, att_grad[at], *tables))
    if seqs == 1:
        return outs[0]
    return (
        jnp.concatenate([o[0] for o in outs]),
        jnp.concatenate([o[1] for o in outs]),
        sum(o[2] for o in outs),
    )


def local(
    tokens,
    cotangent,
    qkv_weight,
    qkv_bias,
    out_weight,
    out_bias,
    up_weight,
    up_bias,
    down_weight,
    down_bias,
    attn_gain,
    attn_shift,
    mlp_gain,
    mlp_shift,
):
    tp_count = lax.axis_size("tp")
    tp_index = lax.axis_index("tp")
    own_rows, width = tokens.shape
    cols = qkv_weight.shape[2]
    units = up_weight.shape[1]
    heads = cols // HD
    scale = HD ** (-0.5)
    all_tokens, grad_rows = (
        lax.all_gather(tokens, "tp", axis=0, tiled=True),
        lax.all_gather(cotangent, "tp", axis=0, tiled=True),
    )
    all_hat, all_factor = norm_rows(all_tokens.astype(jnp.float32))
    first_norm = (all_hat * attn_gain + attn_shift).astype(jnp.bfloat16)
    second_norm = (all_hat * mlp_gain + mlp_shift).astype(jnp.bfloat16)
    flat_qkv = qkv_weight.reshape(qkv_weight.shape[0], 3 * cols)

    flat_bias = qkv_bias.reshape(1, 3 * cols)
    qkv_all = lax.all_gather(flat_qkv, "fsdp", axis=0, tiled=True)
    out_all = lax.all_gather(out_weight, "fsdp", axis=0, tiled=True)
    up_all = lax.all_gather(up_weight, "fsdp", axis=0, tiled=True)
    down_all = lax.all_gather(down_weight, "fsdp", axis=0, tiled=True)
    att_grad16 = jnp.dot(grad_rows, out_all, preferred_element_type=jnp.float32).astype(jnp.bfloat16)
    joined = jnp.dot(first_norm, qkv_all, preferred_element_type=jnp.float32)
    attended, joined_grad, joined_sums = attention(joined, flat_bias, att_grad16, scale)
    up_pre = jnp.dot(second_norm, up_all, preferred_element_type=jnp.float32) + up_bias
    phi = 0.5 + 0.5 * lax.erf(up_pre * (0.5**0.5))
    activated = (up_pre * phi).astype(jnp.bfloat16)
    slope = phi + up_pre * jnp.exp(-0.5 * up_pre * up_pre) * ((0.5 / np.pi) ** 0.5)
    act_grad = jnp.dot(grad_rows, down_all, preferred_element_type=jnp.float32)
    pre_grad16 = (act_grad * slope).astype(jnp.bfloat16)
    block = lax.dot_general(attended, out_all, LAST, preferred_element_type=jnp.float32)
    block = block + lax.dot_general(activated, down_all, LAST, preferred_element_type=jnp.float32)
    branch = lax.psum_scatter(block, "tp", scatter_dimension=0, tiled=True)
    mixed = (tokens.astype(jnp.float32) + branch + (out_bias + down_bias)).astype(jnp.bfloat16)
    shard_rows = qkv_weight.shape[0]

    def cross(left, right):
        return lax.dot_general(left, right, FIRST, preferred_element_type=jnp.float32)

    def scattered(value):
        return lax.psum_scatter(
            value.astype(jnp.bfloat16), "fsdp", scatter_dimension=0, tiled=True
        ).astype(jnp.float32)

    up_weight_grad = scattered(cross(second_norm, pre_grad16))
    down_weight_grad = scattered(cross(grad_rows, activated))
    out_weight_grad = scattered(cross(grad_rows, attended))
    qkv_weight_grad = scattered(cross(first_norm, joined_grad)).reshape(shard_rows, 3, cols)
    first_block = lax.dot_general(joined_grad, qkv_all, LAST, preferred_element_type=jnp.float32)
    second_block = lax.dot_general(pre_grad16, up_all, LAST, preferred_element_type=jnp.float32)
    grad_own = cotangent.astype(jnp.float32)
    gain_terms = jnp.stack(
        [
            jnp.sum(first_block * all_hat, axis=0),
            jnp.sum(first_block, axis=0),
            jnp.sum(second_block * all_hat, axis=0),
            jnp.sum(second_block, axis=0),
            jnp.sum(grad_own, axis=0),
        ]
    )
    hat_grad = lax.psum_scatter(
        first_block * attn_gain + second_block * mlp_gain, "tp", scatter_dimension=0, tiled=True
    )
    hat_own = lax.dynamic_slice_in_dim(all_hat, tp_index * own_rows, own_rows, 0)
    factor_own = lax.dynamic_slice_in_dim(all_factor, tp_index * own_rows, own_rows, 0)
    center_grad = (
        hat_grad
        - jnp.mean(hat_grad, axis=-1, keepdims=True)
        - hat_own * jnp.mean(hat_grad * hat_own, axis=-1, keepdims=True)
    )
    tokens_grad = (grad_own + factor_own * center_grad).astype(jnp.bfloat16)
    qkv_bias_own = joined_sums.reshape(3, cols)
    up_bias_own = jnp.sum(pre_grad16, axis=0, dtype=jnp.float32)
    qkv_spread = lax.dynamic_update_slice_in_dim(
        jnp.zeros((3, width), jnp.float32), qkv_bias_own, tp_index * cols, 1
    )
    up_spread = lax.dynamic_update_slice_in_dim(
        jnp.zeros((units * tp_count,), jnp.float32), up_bias_own, tp_index * units, 0
    )
    gain_total, qkv_total, up_total = lax.psum((gain_terms, qkv_spread, up_spread), ("fsdp", "tp"))
    qkv_bias_grad = lax.dynamic_slice_in_dim(qkv_total, tp_index * cols, cols, 1)
    up_bias_grad = lax.dynamic_slice_in_dim(up_total, tp_index * units, units, 0)
    return (
        mixed,
        tokens_grad,
        qkv_weight_grad,
        qkv_bias_grad,
        out_weight_grad,
        gain_total[4],
        up_weight_grad,
        up_bias_grad,
        down_weight_grad,
        gain_total[4],
        gain_total[0],
        gain_total[1],
        gain_total[2],
        gain_total[3],
    )


def solution(mesh):
    return jax.shard_map(
        local,
        mesh=mesh,
        in_specs=(
            P(("fsdp", "tp"), None),
            P(("fsdp", "tp"), None),
            P("fsdp", None, "tp"),
            P(None, "tp"),
            P("fsdp", "tp"),
            P(),
            P("fsdp", "tp"),
            P("tp"),
            P("fsdp", "tp"),
            P(),
            P(),
            P(),
            P(),
            P(),
        ),
        out_specs=(
            P(("fsdp", "tp"), None),
            P(("fsdp", "tp"), None),
            P("fsdp", None, "tp"),
            P(None, "tp"),
            P("fsdp", "tp"),
            P(),
            P("fsdp", "tp"),
            P("tp"),
            P("fsdp", "tp"),
            P(),
            P(),
            P(),
            P(),
            P(),
        ),
        check_vma=False,
    )
```

```python
import functools

import jax
import jax.numpy as jnp
import numpy as np
from jax import lax
from jax.experimental import pallas as pl
from jax.experimental.pallas import tpu as pltpu
from jax.sharding import PartitionSpec as P

HD = 64
ROT = 16
SEQ = 1024
QBLOCK = 256


EPS = 1e-05
MASKED = -1e30
BASE = 10000.0
LAST = (((1,), (1,)), ((), ()))
FIRST = (((0,), (0,)), ((), ()))


def norm_rows(values):
    center = values - jnp.mean(values, axis=-1, keepdims=True)
    spread = jnp.mean(center * center, axis=-1, keepdims=True)
    factor = lax.rsqrt(spread + EPS)
    return (center * factor, factor)


def rotary_tables():
    half = ROT // 2
    rates = BASE ** (-2.0 * np.arange(half) / ROT)
    angles = np.arange(SEQ)[:, None] * rates[None, :]
    cosine = np.ones((SEQ, HD), np.float32)
    right = np.zeros((SEQ, HD), np.float32)
    left = np.zeros((SEQ, HD), np.float32)
    cosine[:, :half] = cosine[:, half:ROT] = np.cos(angles)
    right[:, :half] = -np.sin(angles)
    left[:, half:ROT] = np.sin(angles)
    return tuple(np.concatenate([one, one], axis=1) for one in (cosine, right, left))


def attend_kernel(scale, q_ref, k_ref, v_ref, qb_ref, kb_ref, vb_ref, ag_ref, cos_ref, sa_ref, sb_ref,
                  att_ref, jg_ref, bias_ref, q_s, k_s, v_s, dk_s, dv_s, dq_s):
    pair = pl.program_id(0)
    cols = jg_ref.shape[1] // 3
    half = ROT // 2
    lanes = 2 * HD
    block = QBLOCK
    low = lax.broadcasted_iota(jnp.int32, (SEQ, lanes), 1) < HD

    def rotary(x, sign):
        return (
            x * cos_ref[...]
            + sign * (pltpu.roll(x, lanes - half, 1) * sa_ref[...] + pltpu.roll(x, half, 1) * sb_ref[...])
        )

    q = (rotary(q_ref[...] + qb_ref[...], 1.0).astype(jnp.bfloat16) * scale).astype(jnp.bfloat16)
    k = rotary(k_ref[...] + kb_ref[...], 1.0).astype(jnp.bfloat16)
    v = (v_ref[...] + vb_ref[...]).astype(jnp.bfloat16)
    zero = jnp.zeros((SEQ, lanes), jnp.bfloat16)
    q_s[0] = jnp.where(low, q, zero)
    q_s[1] = jnp.where(low, zero, q)
    k_s[0] = jnp.where(low, k, zero)
    k_s[1] = jnp.where(low, zero, k)
    v_s[0] = jnp.where(low, v, zero)
    v_s[1] = jnp.where(low, zero, v)
    ag = ag_ref[...]
    nt = (((1,), (1,)), ((), ()))
    tn = (((0,), (0,)), ((), ()))
    keep = lax.broadcasted_iota(jnp.int32, (block, block), 0) <= lax.broadcasted_iota(
        jnp.int32, (block, block), 1
    )
    low_block = low[:block]
    for part in range(SEQ // block):
        begin, end = part * block, (part + 1) * block
        ag_rows = ag_ref[begin:end, :]
        att = jnp.zeros((block, lanes), jnp.float32)
        dq = jnp.zeros((block, lanes), jnp.float32)
        for head in range(2):
            q_rows = q_s[head, begin:end, :]
            ag_head = jnp.where(low_block if head == 0 else ~low_block, ag_rows, jnp.zeros_like(ag_rows))
            scores = lax.dot_general(k_s[head, :end, :], q_rows, nt, preferred_element_type=jnp.float32)
            diag = jnp.where(keep, scores[begin:end], MASKED)
            scores = diag if part == 0 else jnp.concatenate([scores[:begin], diag], axis=0)
            top = jnp.max(scores, axis=0, keepdims=True)
            expo = jnp.exp(scores - top)
            inverse = 1.0 / jnp.sum(expo, axis=0, keepdims=True)
            probs = expo * inverse
            probs16 = probs.astype(jnp.bfloat16)
            att += lax.dot_general(probs16, v_s[head, :end, :], tn, preferred_element_type=jnp.float32)
            dp = lax.dot_general(v_s[head, :end, :], ag_rows, nt, preferred_element_type=jnp.float32)
            delta = jnp.sum(probs * dp, axis=0, keepdims=True)
            ds = (probs * (dp - delta)).astype(jnp.bfloat16)
            dq += lax.dot_general(ds, k_s[head, :end, :], tn, preferred_element_type=jnp.float32)
            dk = lax.dot_general(ds, q_rows, (((1,), (0,)), ((), ())), preferred_element_type=jnp.float32)
            dv = lax.dot_general(probs16, ag_head, (((1,), (0,)), ((), ())), preferred_element_type=jnp.float32)
            first = head == 0
            if first:
                if begin:
                    dk_s[:begin, :] += dk[:begin]
                    dv_s[:begin, :] += dv[:begin]
                dk_s[begin:end, :] = dk[begin:]
                dv_s[begin:end, :] = dv[begin:]
            else:
                dk_s[:end, :] += dk
                dv_s[:end, :] += dv
        att_ref[begin:end, :] = att.astype(jnp.bfloat16)
        dq_s[begin:end, :] = dq * scale
    grads = (rotary(dq_s[...], -1.0), rotary(dk_s[...], -1.0), dv_s[...])
    for which in range(3):
        value = grads[which].astype(jnp.bfloat16)
        at = pl.ds(pl.multiple_of(which * cols + pair * lanes, lanes), lanes)
        jg_ref[:, at] = value
        bias_ref[which] = jnp.sum(value.astype(jnp.float32), axis=0, keepdims=True)


def attention(joined, bias, att_grad, scale):
    rows, cols = att_grad.shape
    lanes = 2 * HD
    pairs = cols // lanes
    seqs = rows // SEQ
    tables = rotary_tables()

    def part(which):
        return pl.BlockSpec((SEQ, lanes), lambda p: (0, which * pairs + p))

    def bias_part(which):
        return pl.BlockSpec((1, lanes), lambda p: (0, which * pairs + p))

    table = pl.BlockSpec((SEQ, lanes), lambda p: (0, 0))
    big = pltpu.VMEM((2, SEQ, lanes), jnp.bfloat16)
    run = pl.pallas_call(
        functools.partial(attend_kernel, scale),
        grid=(pairs,),
        in_specs=[part(0), part(1), part(2), bias_part(0), bias_part(1), bias_part(2), part(0), table, table, table],
        out_specs=[
            part(0),
            pl.BlockSpec((SEQ, 3 * cols), lambda p: (0, 0)),
            pl.BlockSpec((3, 1, lanes), lambda p: (0, 0, p)),
        ],
        out_shape=[
            jax.ShapeDtypeStruct((SEQ, cols), jnp.bfloat16),
            jax.ShapeDtypeStruct((SEQ, 3 * cols), jnp.bfloat16),
            jax.ShapeDtypeStruct((3, 1, cols), jnp.float32),
        ],
        scratch_shapes=[big, big, big] + [pltpu.VMEM((SEQ, lanes), jnp.float32)] * 3,
        compiler_params=pltpu.CompilerParams(vmem_limit_bytes=40 * 2**20),
        cost_estimate=pl.CostEstimate(
            flops=40 * SEQ * SEQ * cols, bytes_accessed=14 * SEQ * cols, transcendentals=SEQ * SEQ * cols // HD
        ),
        name="attention",
    )
    outs = []
    for s in range(seqs):
        at = slice(s * SEQ, (s + 1) * SEQ)
        j = joined[at]
        outs.append(run(j, j, j, bias, bias, bias, att_grad[at], *tables))
    if seqs == 1:
        return outs[0]
    return (
        jnp.concatenate([o[0] for o in outs]),
        jnp.concatenate([o[1] for o in outs]),
        sum(o[2] for o in outs),
    )


def bits_of(name):
    return (lax.axis_size(name) - 1).bit_length()


def swap(value, name, bit):
    size = lax.axis_size(name)
    return lax.ppermute(value, name, [(i, i ^ (1 << bit)) for i in range(size)])


def own_bit(name, bit):
    return (lax.axis_index(name) >> bit) & 1


def gather_rows(value, name):
    rows, width = value.shape
    count = bits_of(name)
    for step in range(count):
        bit = count - 1 - step
        other = swap(value, name, bit)
        upper = own_bit(name, bit) == 1
        value = jnp.stack([jnp.where(upper, other, value), jnp.where(upper, value, other)], axis=step)
    return value.reshape(rows << count, width)


def after(value, *earlier):
    return lax.optimization_barrier((value,) + earlier)[0]


def halve_send(value, name, bit):
    axis = bits_of(name) - 1 - bit
    mine = own_bit(name, bit)
    kept = lax.dynamic_index_in_dim(value, mine, axis, keepdims=False)
    sent = lax.dynamic_index_in_dim(value, 1 - mine, axis, keepdims=False)
    return kept, swap(sent.astype(jnp.bfloat16), name, bit)


class Scatter:
    def __init__(self, value, name, carry):
        self.name, self.carry, self.bit = name, carry, 0
        self.count = bits_of(name)
        rows, width = value.shape
        self.value = value.reshape((2,) * self.count + (rows >> self.count, width))
        self.send()

    def send(self):
        self.kept, self.got = halve_send(self.value, self.name, self.bit)
        self.bit += 1

    def step(self, *earlier):
        if self.bit > self.count:
            return
        got = after(self.got, *earlier) if earlier else self.got
        value = self.kept.astype(jnp.float32) + got.astype(jnp.float32)
        if self.bit < self.count:
            self.value = value.astype(self.carry)
            self.send()
        else:
            self.value = value
            self.bit += 1

    def result(self, *earlier):
        while self.bit <= self.count:
            self.step(*earlier)
        return self.value


def sum_over(value, name):
    for bit in range(bits_of(name)):
        value = value + swap(value, name, bit)
    return value


def local(
    tokens,
    cotangent,
    qkv_weight,
    qkv_bias,
    out_weight,
    out_bias,
    up_weight,
    up_bias,
    down_weight,
    down_bias,
    attn_gain,
    attn_shift,
    mlp_gain,
    mlp_shift,
):
    tp_index = lax.axis_index("tp")
    own_rows, width = tokens.shape
    cols = qkv_weight.shape[2]
    units = up_weight.shape[1]
    heads = cols // HD
    scale = HD ** (-0.5)
    all_tokens, grad_rows = (
        gather_rows(tokens, "tp"),
        gather_rows(cotangent, "tp"),
    )
    all_hat, all_factor = norm_rows(all_tokens.astype(jnp.float32))
    first_norm = (all_hat * attn_gain + attn_shift).astype(jnp.bfloat16)
    second_norm = (all_hat * mlp_gain + mlp_shift).astype(jnp.bfloat16)
    flat_qkv = qkv_weight.reshape(qkv_weight.shape[0], 3 * cols)

    flat_bias = qkv_bias.reshape(1, 3 * cols)
    first_all = lax.all_gather(
        jnp.concatenate([flat_qkv, out_weight], axis=1), "fsdp", axis=0, tiled=True
    )
    second_all = lax.all_gather(
        jnp.concatenate([up_weight, down_weight], axis=1), "fsdp", axis=0, tiled=True
    )
    qkv_all, out_all = first_all[:, : 3 * cols], first_all[:, 3 * cols :]
    up_all, down_all = second_all[:, :units], second_all[:, units:]

    def cross(left, right):
        return lax.dot_general(left, right, FIRST, preferred_element_type=jnp.float32).astype(
            jnp.bfloat16
        )

    att_grad16 = jnp.dot(grad_rows, out_all, preferred_element_type=jnp.float32).astype(jnp.bfloat16)
    joined = jnp.dot(first_norm, qkv_all, preferred_element_type=jnp.float32)
    attended, joined_grad, joined_sums = attention(joined, flat_bias, att_grad16, scale)
    first = Scatter(
        jnp.concatenate([cross(first_norm, joined_grad), cross(grad_rows, attended)], axis=1),
        "fsdp",
        jnp.bfloat16,
    )
    first_block = lax.dot_general(joined_grad, qkv_all, LAST, preferred_element_type=jnp.float32)
    first.step(first_block)
    up_pre = jnp.dot(second_norm, up_all, preferred_element_type=jnp.float32) + up_bias
    phi = 0.5 + 0.5 * lax.erf(up_pre * (0.5**0.5))
    activated = (up_pre * phi).astype(jnp.bfloat16)
    slope = phi + up_pre * jnp.exp(-0.5 * up_pre * up_pre) * ((0.5 / np.pi) ** 0.5)
    down_cross = cross(grad_rows, activated)
    down_weight_grad = lax.psum_scatter(down_cross, "fsdp", scatter_dimension=0, tiled=True).astype(
        jnp.float32
    )
    first.step(down_cross)
    act_grad = jnp.dot(after(grad_rows, down_cross), down_all, preferred_element_type=jnp.float32)
    pre_grad16 = (act_grad * slope).astype(jnp.bfloat16)
    up_cross = cross(second_norm, pre_grad16)
    up = Scatter(up_cross, "fsdp", jnp.bfloat16)
    first.step(up_cross)
    up_bias_own = jnp.sum(pre_grad16, axis=0, dtype=jnp.float32)
    second_block = lax.dot_general(
        after(pre_grad16, up.got), up_all, LAST, preferred_element_type=jnp.float32
    )
    up.step()
    hat_terms = Scatter(first_block * attn_gain + second_block * mlp_gain, "tp", jnp.float32)
    first.step(second_block)
    block = lax.dot_general(
        after(attended, second_block), out_all, LAST, preferred_element_type=jnp.float32
    )
    block = block + lax.dot_general(activated, down_all, LAST, preferred_element_type=jnp.float32)
    branch_terms = Scatter(block, "tp", jnp.float32)
    up.step(block)
    grad_own = cotangent.astype(jnp.float32)
    gain_terms = jnp.stack(
        [
            jnp.sum(first_block * all_hat, axis=0),
            jnp.sum(first_block, axis=0),
            jnp.sum(second_block * all_hat, axis=0),
            jnp.sum(second_block, axis=0),
            jnp.sum(grad_own, axis=0),
        ]
    )
    small = sum_over(
        jnp.concatenate([gain_terms.reshape(-1), joined_sums.reshape(-1), up_bias_own]), "fsdp"
    )
    gain_total = sum_over(small[: 5 * width], "tp").reshape(5, width)
    qkv_bias_grad = small[5 * width : 5 * width + 3 * cols].reshape(3, cols)
    up_bias_grad = small[5 * width + 3 * cols :]
    hat_grad = hat_terms.result(gain_terms)
    hat_own = lax.dynamic_slice_in_dim(all_hat, tp_index * own_rows, own_rows, 0)
    factor_own = lax.dynamic_slice_in_dim(all_factor, tp_index * own_rows, own_rows, 0)
    center_grad = (
        hat_grad
        - jnp.mean(hat_grad, axis=-1, keepdims=True)
        - hat_own * jnp.mean(hat_grad * hat_own, axis=-1, keepdims=True)
    )
    tokens_grad = (grad_own + factor_own * center_grad).astype(jnp.bfloat16)
    branch = branch_terms.result(gain_terms)
    mixed = (tokens.astype(jnp.float32) + branch + (out_bias + down_bias)).astype(jnp.bfloat16)
    shard_rows = qkv_weight.shape[0]
    first_sums = first.result(gain_terms)
    up_weight_grad = up.result(gain_terms)
    qkv_weight_grad = first_sums[:, : 3 * cols].reshape(shard_rows, 3, cols)
    out_weight_grad = first_sums[:, 3 * cols :]
    return (
        mixed,
        tokens_grad,
        qkv_weight_grad,
        qkv_bias_grad,
        out_weight_grad,
        gain_total[4],
        up_weight_grad,
        up_bias_grad,
        down_weight_grad,
        gain_total[4],
        gain_total[0],
        gain_total[1],
        gain_total[2],
        gain_total[3],
    )


def solution(mesh):
    return jax.shard_map(
        local,
        mesh=mesh,
        in_specs=(
            P(("fsdp", "tp"), None),
            P(("fsdp", "tp"), None),
            P("fsdp", None, "tp"),
            P(None, "tp"),
            P("fsdp", "tp"),
            P(),
            P("fsdp", "tp"),
            P("tp"),
            P("fsdp", "tp"),
            P(),
            P(),
            P(),
            P(),
            P(),
        ),
        out_specs=(
            P(("fsdp", "tp"), None),
            P(("fsdp", "tp"), None),
            P("fsdp", None, "tp"),
            P(None, "tp"),
            P("fsdp", "tp"),
            P(),
            P("fsdp", "tp"),
            P("tp"),
            P("fsdp", "tp"),
            P(),
            P(),
            P(),
            P(),
            P(),
        ),
        check_vma=False,
    )
```
